256 devices in a mesh: grp: 64 (over y_lo, x, z), rep: 4 (over y_hi, core).
Axes of the slice: x: 4, y: 4 (y_hi: 2, y_lo: 2; y = y_hi * 2 + y_lo), z: 8, core: 2. Of those that a mesh axis runs over, the one named last changes fastest.
Arguments:
- deviation: float32 [256, 6, 256], P('grp'), may hold values from -6 to 6
- source: float32 [256, 6, 256], P('grp'), may hold values from -6 to 6
- lifetime: float32 [256, 256], P('grp'), may hold values from 0.3 to 3
- rates: float32 [256, 20, 256, 256], P('grp', 'rep'), may hold values from -0.15625 to 0.15625
- partner: int32 [256, 20], P('grp', 'rep'), may hold values from 192 to 255, as said below
- count: int32 [256, 4], P('grp', 'rep'), may hold values from 1 to 5, as said below
Outputs:
- new_deviation: float32 [256, 6, 256], P('grp')
The draws below stay inside these ranges and needn't reach their ends.
Inputs may be any that keep to these rules, and one draw needn't show every extreme that they name: Every partner is a phonon block. Slots k < count of a share are live, the others are ignored.
All inputs are finite; a program needn't handle non-finite values.
Results may differ from the reference program's by a relative error of at most 0.0003.
Values sent between devices are 32-bit elements; how exact they have to be, the bound alone decides.
No kernel may reach another device: no remote copies, remote signals or barrier semaphores. Data moves between devices by JAX's collectives and lax.ppermute only.
A program may use at most 64 MiB of HBM per device.

```python
import math
import jax
import jax.numpy as jnp
from jax import lax

B = 256
C = 6
KR = 5
BLK = 4
NB = 256
NEB = 192
NPB = 64
KTOT = 20
N_GRP = 64


def draw_count(key, part):
    key = jax.random.fold_in(key, 7)
    keys = jax.random.split(key, 3)
    shape = (NB, KTOT // KR)
    first = jax.random.randint(keys[0], shape, 1, KR + 1)
    second = jax.random.randint(keys[1], shape, 1, KR + 1)
    third = jax.random.randint(keys[2], shape, 1, KR + 1)
    least = jnp.minimum(jnp.minimum(first, second), third)
    row_ids = jnp.arange(NB, dtype=jnp.int32)[:, None]
    return jnp.where(row_ids % 29 == 3, KR, least).astype(jnp.int32)


def draw_partner(key, part):
    key = jax.random.fold_in(key, 11)
    keys = jax.random.split(key, 3)
    listed = jax.random.randint(keys[0], (NB, KTOT), 0, NPB)
    row_ids = jnp.arange(NB, dtype=jnp.int32)
    owner = row_ids // BLK
    owners = N_GRP // 4
    first_pick = owner % owners * BLK + jax.random.randint(keys[1], (NB,), 0, BLK)
    second_pick = (owner - 1) % owners * BLK + jax.random.randint(keys[2], (NB,), 0, BLK)
    listed = listed.at[:, 0].set(first_pick)
    listed = listed.at[:, KR].set(second_pick)
    result = NEB + listed
    return result.astype(jnp.int32)


def shard_levels(rng, shape, cuts, low, high):
    def one(axis_at, parts):
        steps = jax.random.uniform(jax.random.fold_in(jax.random.fold_in(rng, 6), axis_at), (parts,), jnp.float32, low / len(cuts), high / len(cuts))
        return jnp.repeat(jnp.exp(steps), shape[axis_at] // parts).reshape((-1,) + (1,) * (len(shape) - axis_at - 1))

    factor_of = one(*cuts[0])
    for cut in cuts[1:]:
        factor_of = factor_of * one(*cut)
    return factor_of


def bell_draw(stream_key, dims, scale, bound, shards=(), kind=jnp.bfloat16):
    level = shard_levels(stream_key, dims, shards, -0.22, 0.18) if shards else 1.0
    array = jax.random.normal(stream_key, dims, jnp.float32) * scale * level
    return jnp.minimum(jnp.maximum(array, -bound), bound).astype(kind)


def setup_inputs(seed: int = 0) -> dict:
    key_list = jax.random.split(jax.random.key(seed), 7)
    return {
        "deviation": bell_draw(key_list[0], (NB, C, B), 1.0, 6.0, ((0, 64),), jnp.float32),
        "source": bell_draw(key_list[1], (NB, C, B), 1.0, 6.0, ((0, 64),), jnp.float32),
        "lifetime": jnp.clip(jnp.exp(math.log(3.0) - 2.3025851 * jax.random.uniform(key_list[2], (NB, B), jnp.float32) ** shard_levels(key_list[2], (NB, B), ((0, 64),), -0.2, 0.2)), 0.3, 3.0),
        "rates": bell_draw(key_list[3], (NB, KTOT, B, B), (B * KR) ** -0.5, 0.15625, ((0, 64), (1, 4)), jnp.float32),
        "partner": draw_partner(jax.random.fold_in(key_list[6], 71), 0),
        "count": draw_count(jax.random.fold_in(key_list[6], 71), 0),
    }


def reference(deviation, source, lifetime, rates, partner, count):
    slot_ids = jnp.arange(KTOT, dtype=jnp.int32)

    def per_block(block_id):
        block_rates = rates[block_id]
        partner_row = partner[block_id]
        live_mask = ((slot_ids % KR) < count[block_id][slot_ids // KR]).astype(jnp.float32)
        picked = deviation[partner_row] * live_mask[:, None, None]
        forward = jnp.einsum("kij,kcj->ci", block_rates, picked, precision=lax.Precision.HIGHEST)
        electron = (block_id < NEB).astype(jnp.float32)
        spread = jnp.einsum("kij,ci->kcj", block_rates, deviation[block_id], precision=lax.Precision.HIGHEST)
        spread = spread * (live_mask * electron)[:, None, None]
        return forward, spread

    forward, spread = lax.map(per_block, jnp.arange(NB, dtype=jnp.int32))
    drag_sum = jax.ops.segment_sum(spread.reshape(NB * KTOT, C, B), partner.reshape(NB * KTOT), num_segments=NB)
    summed = forward + drag_sum
    return source + lifetime[:, None, :] * summed
```

```python
import jax
import jax.numpy as jnp
from jax import lax
from jax.experimental import pallas as pl
from jax.experimental.pallas import tpu as pltpu
from jax.sharding import PartitionSpec as P

Y_LO, X_HIGH, Y_HI, CORE = 128, 64, 2, 1
DEVICES = 256
BLOCKS, SLOTS, COMPONENTS, STATES, HALF = 4, 5, 6, 256, 128
PHONON = 64
FIRST_PHONON = 192
ROWS = BLOCKS * COMPONENTS
OWNERS = PHONON // BLOCKS
QUARTERS = [[quarter * OWNERS + owner for owner in range(OWNERS)] for quarter in range(4)]


def swap(value, bit):
    return lax.ppermute(value, ("grp", "rep"), [(i, i ^ bit) for i in range(DEVICES)])


def push(value, bit, towards, also=0):
    pairs = [
        (i, i ^ bit) for i in range(DEVICES) if ((i ^ bit) & bit != 0) == towards and i & also == also
    ]
    return lax.ppermute(value, ("grp", "rep"), pairs)


def split(value):
    high = value.astype(jnp.bfloat16)
    low = (value - high.astype(jnp.float32)).astype(jnp.bfloat16)
    return high, low


def stack_split(value):
    padded = jnp.concatenate([value, jnp.zeros((2, value.shape[1]), jnp.float32)], axis=0)
    high, low = split(padded)
    both = jnp.concatenate([high.astype(jnp.float32), low.astype(jnp.float32)], axis=0)
    return high, both.astype(jnp.bfloat16)


def product(high, both, weights, contract):
    dims = (((1,), (contract,)), ((), ()))
    rates_high, rates_low = split(weights)
    main = lax.dot_general(both, rates_high, dims, preferred_element_type=jnp.float32)
    rest = lax.dot_general(high, rates_low, dims, preferred_element_type=jnp.float32)
    return main[:8] + main[8:] + rest


def fetch(rates, held, sems, block, slot):
    return pltpu.make_async_copy(
        rates.at[block, slot], held.at[block * SLOTS + slot], sems.at[block * SLOTS + slot]
    )


def start_fetches(count, rates, held, sems):
    for block in range(BLOCKS):

        @pl.loop(0, count[block])
        def _(slot):
            fetch(rates, held, sems, block, slot).start()


def spread_kernel(count, target, deviation, rates, out, held, sems):
    start_fetches(count, rates, held, sems)
    out[...] = jnp.zeros_like(out)
    for block in range(BLOCKS):
        high, both = stack_split(deviation[block])

        @pl.loop(0, count[block])
        def _(slot):
            fetch(rates, held, sems, block, slot).wait()
            value = product(high, both, held[block * SLOTS + slot], 0)
            row = target[block * SLOTS + slot] * COMPONENTS
            out[0, pl.ds(row, COMPONENTS), :] += value[:COMPONENTS, :HALF]
            out[1, pl.ds(row, COMPONENTS), :] += value[:COMPONENTS, HALF:]


def forward_kernel(count, target, phonon, rates, out, held, sems):
    start_fetches(count, rates, held, sems)
    for block in range(BLOCKS):

        def visit(slot, total):
            fetch(rates, held, sems, block, slot).wait()
            row = target[block * SLOTS + slot] * COMPONENTS
            picked = jnp.concatenate(
                [phonon[0, pl.ds(row, COMPONENTS), :], phonon[1, pl.ds(row, COMPONENTS), :]], axis=1
            )
            high, both = stack_split(picked)
            return total + product(high, both, held[block * SLOTS + slot], 1)

        total = lax.fori_loop(0, count[block], visit, jnp.zeros((8, STATES), jnp.float32))
        for half in range(2):
            out[half, block * COMPONENTS : (block + 1) * COMPONENTS, :] = total[
                :COMPONENTS, half * HALF : (half + 1) * HALF
            ]


def rate_kernel(body, name, rows):
    smem = pl.BlockSpec(memory_space=pltpu.SMEM)
    vmem = pl.BlockSpec(memory_space=pltpu.VMEM)
    return pl.pallas_call(
        body,
        name=name,
        out_shape=jax.ShapeDtypeStruct((2, rows, HALF), jnp.float32),
        in_specs=[smem, smem, vmem, pl.BlockSpec(memory_space=pl.ANY)],
        out_specs=vmem,
        scratch_shapes=[
            pltpu.VMEM((BLOCKS * SLOTS, STATES, STATES), jnp.float32),
            pltpu.SemaphoreType.DMA((BLOCKS * SLOTS,)),
        ],
        compiler_params=pltpu.CompilerParams(vmem_limit_bytes=24 * 1024 * 1024),
        cost_estimate=pl.CostEstimate(
            flops=6 * BLOCKS * SLOTS * 8 * STATES * STATES,
            bytes_accessed=BLOCKS * SLOTS * STATES * STATES * 4,
            transcendentals=0,
        ),
    )


def on_device(deviation, source, lifetime, rates, partner, count):
    grp = lax.axis_index("grp")
    core = lax.axis_index("rep") % 2
    is_phonon = grp >= 3 * OWNERS
    target = (partner - FIRST_PHONON).reshape(-1)
    live = count[:, 0]

    def half_of(value):
        return lax.dynamic_index_in_dim(value, core, 0, keepdims=False)

    def other_of(value):
        return lax.dynamic_index_in_dim(value, 1 - core, 0, keepdims=False)

    def both_halves(mine, other):
        return jnp.stack([jnp.where(core == 0, mine, other), jnp.where(core == 0, other, mine)])

    own = lax.dynamic_slice_in_dim(deviation, core * HALF, HALF, 2).reshape(ROWS, HALF)
    from_phonon = push(own, Y_LO, False, also=Y_LO + X_HIGH)
    at_x_high = jnp.where(is_phonon, own, from_phonon)
    from_x_high = push(at_x_high, X_HIGH, False)
    has_x_high = (grp // OWNERS) % 2 == 1
    carried = jnp.where(has_x_high, at_x_high, from_x_high)

    spread_live = jnp.where(is_phonon, 0, live)
    spread = rate_kernel(spread_kernel, "spread", PHONON * COMPONENTS)(
        spread_live, target, deviation, rates
    )
    drag = half_of(spread) + swap(other_of(spread), CORE)

    parcel = jnp.concatenate(
        [drag.reshape(OWNERS, ROWS, HALF), jnp.broadcast_to(carried, (OWNERS, ROWS, HALF))], axis=1
    )
    arrived = lax.all_to_all(parcel, "grp", 0, 0, axis_index_groups=QUARTERS, tiled=True)
    drag = arrived[:, :ROWS].sum(0)
    phonon_half = arrived[:, ROWS:].reshape(PHONON * COMPONENTS, HALF)

    phonon = both_halves(phonon_half, swap(phonon_half, CORE))
    forward = rate_kernel(forward_kernel, "forward", ROWS)(live, target, phonon, rates)
    forward = half_of(forward) + swap(other_of(forward), CORE)

    drag = drag + push(drag, Y_LO, True)
    drag = drag + push(drag, X_HIGH, True)
    total = forward + jnp.where(is_phonon, drag, 0.0)
    total = total + swap(total, Y_HI)
    halves = both_halves(total, swap(total, CORE)).reshape(2, BLOCKS, COMPONENTS, HALF)
    summed = jnp.concatenate([halves[0], halves[1]], axis=-1)
    return source + lifetime[:, None, :] * summed


def solution(mesh):
    placed = (
        P("grp", None, None),
        P("grp", None, None),
        P("grp", None),
        P("grp", "rep", None, None),
        P("grp", "rep"),
        P("grp", "rep"),
    )
    return jax.shard_map(
        on_device, mesh=mesh, in_specs=placed, out_specs=P("grp", None, None), check_vma=False
    )
```

```python
import jax
import jax.numpy as jnp
from jax import lax
from jax.experimental import pallas as pl
from jax.experimental.pallas import tpu as pltpu
from jax.sharding import PartitionSpec as P

Y_LO, X_HIGH, Y_HI, CORE = 128, 64, 2, 1
QUARTER_BITS = Y_LO + X_HIGH
DEVICES = 256
BLOCKS, SLOTS, COMPONENTS, STATES, HALF = 4, 5, 6, 256, 128
PAIRS = BLOCKS * SLOTS
PHONON = 64
FIRST_PHONON = 192
ROWS = BLOCKS * COMPONENTS
OWNERS = PHONON // BLOCKS
QUARTERS = [[quarter * OWNERS + owner for owner in range(OWNERS)] for quarter in range(4)]


def swap(value, bit):
    return lax.ppermute(value, ("grp", "rep"), [(i, i ^ bit) for i in range(DEVICES)])


def from_phonon(value, bits):
    pairs = [(i, i ^ bits) for i in range(DEVICES) if i & QUARTER_BITS == QUARTER_BITS]
    return lax.ppermute(value, ("grp", "rep"), pairs)


def to_phonon(value, bits):
    pairs = [(i ^ bits, i) for i in range(DEVICES) if i & QUARTER_BITS == QUARTER_BITS]
    return lax.ppermute(value, ("grp", "rep"), pairs)


def split(value):
    high = value.astype(jnp.bfloat16)
    low = (value - high.astype(jnp.float32)).astype(jnp.bfloat16)
    return high, low


def stack_split(value):
    padded = jnp.concatenate([value, jnp.zeros((2, value.shape[1]), jnp.float32)], axis=0)
    high, low = split(padded)
    both = jnp.concatenate([high.astype(jnp.float32), low.astype(jnp.float32)], axis=0)
    return high, both.astype(jnp.bfloat16)


def product(high, both, weights, contract):
    rates_high, rates_low = split(weights)
    dims = (((1,), (contract,)), ((), ()))
    main = lax.dot_general(both, rates_high, dims, preferred_element_type=jnp.float32)
    rest = lax.dot_general(high, rates_low, dims, preferred_element_type=jnp.float32)
    return main[:8] + main[8:] + rest


def rate_copies(count_hbm, partner_hbm, rates, count, partner, held, sems, small_sems):
    def fetch(block, slot):
        pair = block * SLOTS + slot
        return pltpu.make_async_copy(rates.at[block, slot], held.at[pair], sems.at[pair])

    counts = pltpu.make_async_copy(count_hbm, count, small_sems.at[0])
    partners = pltpu.make_async_copy(partner_hbm, partner, small_sems.at[1])
    counts.start()
    partners.start()
    for block in range(BLOCKS):
        fetch(block, 0).start()
    counts.wait()
    for block in range(BLOCKS):

        @pl.loop(1, count[0, block])
        def _(slot):
            fetch(block, slot).start()

    partners.wait()
    return fetch


def spread_kernel(
    count_hbm, partner_hbm, deviation, rates, keep, give, own, held, count, partner, own_sem, sems, small
):
    keep[...] = jnp.zeros_like(keep)
    give[...] = jnp.zeros_like(give)
    is_electron = lax.axis_index("grp") < 3 * OWNERS
    core = lax.rem(lax.axis_index("rep"), 2)

    @pl.when(is_electron)
    def _():
        own_copy = pltpu.make_async_copy(deviation, own, own_sem)
        own_copy.start()
        fetch = rate_copies(count_hbm, partner_hbm, rates, count, partner, held, sems, small)
        own_copy.wait()
        for block in range(BLOCKS):
            rows = [own[component, block : block + 1, :] for component in range(COMPONENTS)]
            high, both = stack_split(jnp.concatenate(rows, axis=0))

            @pl.loop(0, count[0, block])
            def _(slot):
                fetch(block, slot).wait()
                value = product(high, both, held[block * SLOTS + slot], 0)[:COMPONENTS]
                left, right = value[:, :HALF], value[:, HALF:]
                row = (partner[block, slot] - FIRST_PHONON) * COMPONENTS
                keep[pl.ds(row, COMPONENTS), :] += jnp.where(core == 0, left, right)
                give[pl.ds(row, COMPONENTS), :] += jnp.where(core == 0, right, left)


def forward_kernel(
    count_hbm, partner_hbm, mine, other, rates, keep, give, held, count, partner, sems, small
):
    core = lax.rem(lax.axis_index("rep"), 2)
    fetch = rate_copies(count_hbm, partner_hbm, rates, count, partner, held, sems, small)
    for block in range(BLOCKS):

        def visit(slot, total):
            fetch(block, slot).wait()
            row = (partner[block, slot] - FIRST_PHONON) * COMPONENTS
            near, far = mine[pl.ds(row, COMPONENTS), :], other[pl.ds(row, COMPONENTS), :]
            left, right = jnp.where(core == 0, near, far), jnp.where(core == 0, far, near)
            high, both = stack_split(jnp.concatenate([left, right], axis=1))
            return total + product(high, both, held[block * SLOTS + slot], 1)

        total = lax.fori_loop(0, count[0, block], visit, jnp.zeros((8, STATES), jnp.float32))
        left, right = total[:COMPONENTS, :HALF], total[:COMPONENTS, HALF:]
        rows = slice(block * COMPONENTS, (block + 1) * COMPONENTS)
        keep[rows, :] = jnp.where(core == 0, left, right)
        give[rows, :] = jnp.where(core == 0, right, left)


VMEM = pl.BlockSpec(memory_space=pltpu.VMEM)
HBM = pl.BlockSpec(memory_space=pltpu.HBM)
RATE_SCRATCH = [
    pltpu.VMEM((PAIRS, STATES, STATES), jnp.float32),
    pltpu.SMEM((1, BLOCKS), jnp.int32),
    pltpu.SMEM((BLOCKS, SLOTS), jnp.int32),
]
RATE_SEMS = [pltpu.SemaphoreType.DMA((PAIRS,)), pltpu.SemaphoreType.DMA((2,))]


def rate_kernel(body, name, rows, in_specs, first_scratch, later_sems):
    return pl.pallas_call(
        body,
        name=name,
        out_shape=[jax.ShapeDtypeStruct((rows, HALF), jnp.float32)] * 2,
        in_specs=in_specs,
        out_specs=[VMEM] * 2,
        scratch_shapes=first_scratch + RATE_SCRATCH + later_sems + RATE_SEMS,
        compiler_params=pltpu.CompilerParams(vmem_limit_bytes=16 * 1024 * 1024),
        cost_estimate=pl.CostEstimate(
            flops=6 * PAIRS * 8 * STATES * STATES,
            bytes_accessed=2 * PAIRS * STATES * STATES * 4,
            transcendentals=0,
        ),
    )


def in_hbm(*values):
    return [pltpu.with_memory_space_constraint(value, pltpu.HBM) for value in values]


def spread(count, partner, deviation, rates):
    own = pltpu.VMEM((COMPONENTS, BLOCKS, STATES), jnp.float32)
    return rate_kernel(
        spread_kernel, "spread", PHONON * COMPONENTS, [HBM] * 4, [own], [pltpu.SemaphoreType.DMA]
    )(*in_hbm(count, partner, deviation, rates))


def forward(count, partner, mine, other, rates):
    count, partner, rates = in_hbm(count, partner, rates)
    return rate_kernel(forward_kernel, "forward", ROWS, [HBM, HBM, VMEM, VMEM, HBM], [], [])(
        count, partner, mine, other, rates
    )


def on_device(deviation, source, lifetime, rates, partner, count):
    core = lax.axis_index("rep") % 2
    is_phonon = lax.axis_index("grp") >= 3 * OWNERS
    live = count.T
    turned = deviation.transpose(1, 0, 2)

    def both_halves(mine, other):
        left, right = jnp.where(core == 0, mine, other), jnp.where(core == 0, other, mine)
        return jnp.concatenate([left, right], axis=-1)

    arrived = [swap(turned, bits) for bits in (QUARTER_BITS, X_HIGH, Y_LO)]
    quarter = lax.axis_index("grp") // OWNERS
    carried = jnp.where(quarter == 0, arrived[0], jnp.where(quarter == 1, arrived[2], arrived[1]))
    carried = jnp.where(is_phonon, turned, carried)
    carried = lax.dynamic_slice_in_dim(carried, core * HALF, HALF, 2)
    carried = carried.transpose(1, 0, 2).reshape(ROWS, HALF)

    keep, give = spread(live, partner, turned, rates)
    drag = keep + swap(give, CORE)

    parcel = jnp.concatenate(
        [drag.reshape(OWNERS, ROWS, HALF), jnp.broadcast_to(carried, (OWNERS, ROWS, HALF))], axis=1
    )
    arrived = lax.all_to_all(parcel, "grp", 0, 0, axis_index_groups=QUARTERS, tiled=True)
    drag = arrived[:, :ROWS].sum(0)
    phonon = arrived[:, ROWS:].reshape(PHONON * COMPONENTS, HALF)

    others = [swap(drag, bits) for bits in (QUARTER_BITS, X_HIGH, Y_LO)]
    keep, give = forward(live, partner, phonon, swap(phonon, CORE), rates)
    total = keep + swap(give, CORE)
    total = total + jnp.where(is_phonon, drag + others[0] + others[1] + others[2], 0.0)
    total = total + swap(total, Y_HI)
    summed = both_halves(total, swap(total, CORE)).reshape(BLOCKS, COMPONENTS, STATES)
    return source + lifetime[:, None, :] * summed


def solution(mesh):
    placed = (
        P("grp", None, None),
        P("grp", None, None),
        P("grp", None),
        P("grp", "rep", None, None),
        P("grp", "rep"),
        P("grp", "rep"),
    )
    return jax.shard_map(
        on_device, mesh=mesh, in_specs=placed, out_specs=P("grp", None, None), check_vma=False
    )
```

```python
import jax
import jax.numpy as jnp
from jax import lax
from jax.experimental import pallas as pl
from jax.experimental.pallas import tpu as pltpu
from jax.sharding import PartitionSpec as P

Y_LO, X_HIGH, Y_HI, CORE = 128, 64, 2, 1
QUARTER_BITS = Y_LO + X_HIGH
DEVICES = 256
BLOCKS, SLOTS, COMPONENTS, STATES, HALF = 4, 5, 6, 256, 128
PAIRS = BLOCKS * SLOTS
UNROLL = 4
PHONON = 64
FIRST_PHONON = 192
ROWS = BLOCKS * COMPONENTS
OWNERS = PHONON // BLOCKS
QUARTERS = [[quarter * OWNERS + owner for owner in range(OWNERS)] for quarter in range(4)]


def swap(value, bit):
    return lax.ppermute(value, ("grp", "rep"), [(i, i ^ bit) for i in range(DEVICES)])


def from_phonon(value, bits):
    pairs = [(i, i ^ bits) for i in range(DEVICES) if i & QUARTER_BITS == QUARTER_BITS]
    return lax.ppermute(value, ("grp", "rep"), pairs)


def to_phonon(value, bits):
    pairs = [(i ^ bits, i) for i in range(DEVICES) if i & QUARTER_BITS == QUARTER_BITS]
    return lax.ppermute(value, ("grp", "rep"), pairs)


def split(value):
    high = value.astype(jnp.bfloat16)
    low = (value - high.astype(jnp.float32)).astype(jnp.bfloat16)
    return high, low


def stack_split(value):
    high, low = split(value)
    both = jnp.concatenate([high.astype(jnp.float32), low.astype(jnp.float32)], axis=0)
    return high, both.astype(jnp.bfloat16)


def product(high, both, weights, contract):
    rates_high, rates_low = split(weights)
    dims = (((1,), (contract,)), ((), ()))
    main = lax.dot_general(both, rates_high, dims, preferred_element_type=jnp.float32)
    rest = lax.dot_general(high, rates_low, dims, preferred_element_type=jnp.float32)
    return main[:8] + main[8:] + rest


def rate_copies(count_hbm, partner_hbm, rates, count, partner, held, sems, small_sems):
    def fetch(block, slot):
        pair = block * SLOTS + slot
        return pltpu.make_async_copy(rates.at[block, slot], held.at[pair], sems.at[pair])

    counts = pltpu.make_async_copy(count_hbm, count, small_sems.at[0])
    partners = pltpu.make_async_copy(partner_hbm, partner, small_sems.at[1])
    counts.start()
    partners.start()
    for block in range(BLOCKS):
        fetch(block, 0).start()
    counts.wait()
    for block in range(BLOCKS):

        @pl.loop(1, count[0, block])
        def _(slot):
            fetch(block, slot).start()

    partners.wait()
    return fetch


def visit_live(count, chosen, fetch, visit):
    total = jnp.int32(0)
    for block in range(BLOCKS):

        def note(slot, at):
            chosen[at] = block * SLOTS + slot
            return at + 1

        total = lax.fori_loop(0, count[0, block], note, total)

    @pl.loop(0, lax.div(total + (UNROLL - 1), UNROLL))
    def _(step):
        places = [step * UNROLL + offset for offset in range(UNROLL)]
        pairs = [chosen[jnp.minimum(place, total - 1)] for place in places]
        blocks = [lax.div(pair, SLOTS) for pair in pairs]
        slots = [pair - SLOTS * block for pair, block in zip(pairs, blocks)]
        for place, block, slot in zip(places, blocks, slots):

            @pl.when(place < total)
            def _():
                fetch(block, slot).wait()

        visit([(block, slot, place < total) for block, slot, place in zip(blocks, slots, places)])


def spread_kernel(
    count_hbm, partner_hbm, deviation, rates, keep, give, own, rows, held, count, partner, chosen, own_sem, sems, small
):
    keep[...] = jnp.zeros_like(keep)
    give[...] = jnp.zeros_like(give)
    core = lax.rem(lax.axis_index("rep"), 2)

    @pl.when(lax.axis_index("grp") < 3 * OWNERS)
    def _():
        own_copy = pltpu.make_async_copy(deviation, own, own_sem)
        own_copy.start()
        fetch = rate_copies(count_hbm, partner_hbm, rates, count, partner, held, sems, small)
        own_copy.wait()
        for block in range(BLOCKS):
            parts = [own[component, block : block + 1, :] for component in range(COMPONENTS)]
            rows[block] = jnp.concatenate(parts + [jnp.zeros((2, STATES), jnp.float32)], axis=0)

        def visit(some):
            values = []
            for block, slot, live in some:
                high, both = stack_split(jnp.where(live, rows[block], 0.0))
                values.append(product(high, both, held[block * SLOTS + slot], 0)[:COMPONENTS])
            for (block, slot, live), value in zip(some, values):
                left, right = value[:, :HALF], value[:, HALF:]
                row = (partner[block, slot] - FIRST_PHONON) * COMPONENTS
                keep[pl.ds(row, COMPONENTS), :] += jnp.where(core == 0, left, right)
                give[pl.ds(row, COMPONENTS), :] += jnp.where(core == 0, right, left)

        visit_live(count, chosen, fetch, visit)


def forward_kernel(
    count_hbm, partner_hbm, mine, other, rates, keep, give, totals, held, count, partner, chosen, sems, small
):
    core = lax.rem(lax.axis_index("rep"), 2)
    fetch = rate_copies(count_hbm, partner_hbm, rates, count, partner, held, sems, small)
    totals[...] = jnp.zeros_like(totals)

    def visit(some):
        values = []
        for block, slot, live in some:
            row = (partner[block, slot] - FIRST_PHONON) * COMPONENTS
            near, far = mine[pl.ds(row, COMPONENTS), :], other[pl.ds(row, COMPONENTS), :]
            left, right = jnp.where(core == 0, near, far), jnp.where(core == 0, far, near)
            picked = jnp.concatenate([left, right], axis=1)
            padded = jnp.concatenate([picked, jnp.zeros((2, STATES), jnp.float32)], axis=0)
            high, both = stack_split(jnp.where(live, padded, 0.0))
            values.append(product(high, both, held[block * SLOTS + slot], 1))
        for (block, slot, live), value in zip(some, values):
            totals[block] += value

    visit_live(count, chosen, fetch, visit)
    for block in range(BLOCKS):
        left, right = totals[block, :COMPONENTS, :HALF], totals[block, :COMPONENTS, HALF:]
        rows = slice(block * COMPONENTS, (block + 1) * COMPONENTS)
        keep[rows, :] = jnp.where(core == 0, left, right)
        give[rows, :] = jnp.where(core == 0, right, left)


VMEM = pl.BlockSpec(memory_space=pltpu.VMEM)
HBM = pl.BlockSpec(memory_space=pltpu.HBM)
RATE_SCRATCH = [
    pltpu.VMEM((PAIRS, STATES, STATES), jnp.float32),
    pltpu.SMEM((1, BLOCKS), jnp.int32),
    pltpu.SMEM((BLOCKS, SLOTS), jnp.int32),
    pltpu.SMEM((PAIRS,), jnp.int32),
]
RATE_SEMS = [pltpu.SemaphoreType.DMA((PAIRS,)), pltpu.SemaphoreType.DMA((2,))]


def rate_kernel(body, name, outs, in_specs, first_scratch, later_sems):
    return pl.pallas_call(
        body,
        name=name,
        out_shape=[jax.ShapeDtypeStruct((rows, HALF), jnp.float32) for rows in outs],
        in_specs=in_specs,
        out_specs=[VMEM] * len(outs),
        scratch_shapes=first_scratch + RATE_SCRATCH + later_sems + RATE_SEMS,
        compiler_params=pltpu.CompilerParams(vmem_limit_bytes=16 * 1024 * 1024),
        cost_estimate=pl.CostEstimate(
            flops=6 * PAIRS * 8 * STATES * STATES,
            bytes_accessed=2 * PAIRS * STATES * STATES * 4,
            transcendentals=0,
        ),
    )


def in_hbm(*values):
    return [pltpu.with_memory_space_constraint(value, pltpu.HBM) for value in values]


def spread(count, partner, deviation, rates):
    outs = [PHONON * COMPONENTS] * 2
    own = pltpu.VMEM((COMPONENTS, BLOCKS, STATES), jnp.float32)
    padded = pltpu.VMEM((BLOCKS, 8, STATES), jnp.float32)
    return rate_kernel(
        spread_kernel, "spread", outs, [HBM] * 4, [own, padded], [pltpu.SemaphoreType.DMA]
    )(*in_hbm(count, partner, deviation, rates))


def forward(count, partner, mine, other, rates):
    count, partner, rates = in_hbm(count, partner, rates)
    totals = pltpu.VMEM((BLOCKS, 8, STATES), jnp.float32)
    return rate_kernel(
        forward_kernel, "forward", [ROWS] * 2, [HBM, HBM, VMEM, VMEM, HBM], [totals], []
    )(count, partner, mine, other, rates)


def on_device(deviation, source, lifetime, rates, partner, count):
    core = lax.axis_index("rep") % 2
    is_phonon = lax.axis_index("grp") >= 3 * OWNERS
    live = count.T
    turned = deviation.transpose(1, 0, 2)

    def both_halves(mine, other):
        left, right = jnp.where(core == 0, mine, other), jnp.where(core == 0, other, mine)
        return jnp.concatenate([left, right], axis=-1)

    arrived = [swap(turned, bits) for bits in (QUARTER_BITS, X_HIGH, Y_LO)]
    quarter = lax.axis_index("grp") // OWNERS
    carried = jnp.where(quarter == 0, arrived[0], jnp.where(quarter == 1, arrived[2], arrived[1]))
    carried = jnp.where(is_phonon, turned, carried)
    carried = lax.dynamic_slice_in_dim(carried, core * HALF, HALF, 2)
    carried = carried.transpose(1, 0, 2).reshape(ROWS, HALF)

    keep, give = spread(live, partner, turned, rates)
    drag = keep + swap(give, CORE)

    parcel = jnp.concatenate(
        [drag.reshape(OWNERS, ROWS, HALF), jnp.broadcast_to(carried, (OWNERS, ROWS, HALF))], axis=1
    )
    arrived = lax.all_to_all(parcel, "grp", 0, 0, axis_index_groups=QUARTERS, tiled=True)
    drag = arrived[:, :ROWS].sum(0)
    phonon = arrived[:, ROWS:].reshape(PHONON * COMPONENTS, HALF)

    others = [swap(drag, bits) for bits in (QUARTER_BITS, X_HIGH, Y_LO)]
    keep, give = forward(live, partner, phonon, swap(phonon, CORE), rates)
    total = keep + swap(give, CORE)
    total = total + jnp.where(is_phonon, drag + others[0] + others[1] + others[2], 0.0)
    total = total + swap(total, Y_HI)
    summed = both_halves(total, swap(total, CORE)).reshape(BLOCKS, COMPONENTS, STATES)
    return source + lifetime[:, None, :] * summed


def solution(mesh):
    placed = (
        P("grp", None, None),
        P("grp", None, None),
        P("grp", None),
        P("grp", "rep", None, None),
        P("grp", "rep"),
        P("grp", "rep"),
    )
    return jax.shard_map(
        on_device, mesh=mesh, in_specs=placed, out_specs=P("grp", None, None), check_vma=False
    )
```

```python
import jax
import jax.numpy as jnp
from jax import lax
from jax.experimental import pallas as pl
from jax.experimental.pallas import tpu as pltpu
from jax.sharding import PartitionSpec as P

Y_LO, X_HIGH, X_LOW, Y_HI, CORE = 128, 64, 32, 2, 1
MIRROR = X_HIGH + X_LOW
QUARTER_BITS = Y_LO + MIRROR
DEVICES = 256
BLOCKS, SLOTS, COMPONENTS, STATES, HALF = 4, 5, 6, 256, 128
PAIRS = BLOCKS * SLOTS
UNROLL = 4
PHONON = 64
FIRST_PHONON = 192
ROWS = BLOCKS * COMPONENTS
OWNERS = PHONON // BLOCKS
QUARTERS = [[quarter * OWNERS + owner for owner in range(OWNERS)] for quarter in range(4)]


def swap(value, bit):
    return lax.ppermute(value, ("grp", "rep"), [(i, i ^ bit) for i in range(DEVICES)])


def from_phonon(value, bits):
    pairs = [(i, i ^ bits) for i in range(DEVICES) if i & QUARTER_BITS == QUARTER_BITS]
    return lax.ppermute(value, ("grp", "rep"), pairs)


def to_phonon(value, bits):
    pairs = [(i ^ bits, i) for i in range(DEVICES) if i & QUARTER_BITS == QUARTER_BITS]
    return lax.ppermute(value, ("grp", "rep"), pairs)


def split(value):
    high = value.astype(jnp.bfloat16)
    low = (value - high.astype(jnp.float32)).astype(jnp.bfloat16)
    return high, low


def stack_split(value):
    high, low = split(value)
    both = jnp.concatenate([high.astype(jnp.float32), low.astype(jnp.float32)], axis=0)
    return high, both.astype(jnp.bfloat16)


def multiply(high, both, rates_high, rates_low, contract):
    dims = (((1,), (contract,)), ((), ()))
    main = lax.dot_general(both, rates_high, dims, preferred_element_type=jnp.float32)
    rest = lax.dot_general(high, rates_low, dims, preferred_element_type=jnp.float32)
    return main[:8] + main[8:] + rest


def product(high, both, weights, contract):
    return multiply(high, both, *split(weights), contract)


def rate_copies(count_hbm, partner_hbm, rates, count, partner, held, sems, small_sems, meanwhile):
    def fetch(block, slot):
        pair = block * SLOTS + slot
        return pltpu.make_async_copy(rates.at[block, slot], held.at[pair], sems.at[pair])

    counts = pltpu.make_async_copy(count_hbm, count, small_sems.at[0])
    partners = pltpu.make_async_copy(partner_hbm, partner, small_sems.at[1])
    counts.start()
    partners.start()
    for block in range(BLOCKS):
        fetch(block, 0).start()
    meanwhile()
    counts.wait()
    for block in range(BLOCKS):

        @pl.loop(1, count[0, block])
        def _(slot):
            fetch(block, slot).start()

    partners.wait()
    return fetch


def visit_live(count, chosen, fetch, visit):
    total = jnp.int32(0)
    for block in range(BLOCKS):

        def note(slot, at):
            chosen[at] = block * SLOTS + slot
            return at + 1

        total = lax.fori_loop(0, count[0, block], note, total)

    @pl.loop(0, lax.div(total + (UNROLL - 1), UNROLL))
    def _(step):
        places = [step * UNROLL + offset for offset in range(UNROLL)]
        pairs = [chosen[jnp.minimum(place, total - 1)] for place in places]
        blocks = [lax.div(pair, SLOTS) for pair in pairs]
        slots = [pair - SLOTS * block for pair, block in zip(pairs, blocks)]
        for place, block, slot in zip(places, blocks, slots):

            if fetch is not None:

                @pl.when(place < total)
                def _():
                    fetch(block, slot).wait()

        visit([(block, slot, place < total) for block, slot, place in zip(blocks, slots, places)])


def spread_kernel(
    count_hbm, partner_hbm, deviation, rates, keep, give, own, rows, held, count, partner, chosen, own_sem, sems, small
):
    core = lax.rem(lax.axis_index("rep"), 2)

    def clear():
        keep[...] = jnp.zeros_like(keep)
        give[...] = jnp.zeros_like(give)

    @pl.when(lax.axis_index("grp") >= 3 * OWNERS)
    def _():
        clear()

    @pl.when(lax.axis_index("grp") < 3 * OWNERS)
    def _():
        own_copy = pltpu.make_async_copy(deviation, own, own_sem)
        own_copy.start()
        fetch = rate_copies(
            count_hbm, partner_hbm, rates, count, partner, held, sems, small, clear
        )
        own_copy.wait()
        for block in range(BLOCKS):
            parts = [own[component, block : block + 1, :] for component in range(COMPONENTS)]
            rows[block] = jnp.concatenate(parts + [jnp.zeros((2, STATES), jnp.float32)], axis=0)

        def visit(some):
            values = []
            for block, slot, live in some:
                high, both = stack_split(jnp.where(live, rows[block], 0.0))
                values.append(product(high, both, held[block * SLOTS + slot], 0)[:COMPONENTS])
            for (block, slot, live), value in zip(some, values):
                left, right = value[:, :HALF], value[:, HALF:]
                row = (partner[block, slot] - FIRST_PHONON) * COMPONENTS
                keep[pl.ds(row, COMPONENTS), :] += jnp.where(core == 0, left, right)
                give[pl.ds(row, COMPONENTS), :] += jnp.where(core == 0, right, left)

        visit_live(count, chosen, fetch, visit)


def prepare_kernel(count_hbm, partner_hbm, rates, high, low, token, held, count, partner, chosen, sems, small):
    def clear():
        token[...] = jnp.zeros_like(token)

    fetch = rate_copies(
        count_hbm, partner_hbm, rates, count, partner, held, sems, small, clear
    )

    def visit(some):
        for block, slot, _ in some:
            pair = block * SLOTS + slot
            high[pair], low[pair] = split(held[pair])

    visit_live(count, chosen, fetch, visit)


def forward_kernel(count_hbm, partner_hbm, mine, other, high_ref, low_ref, drag, out, totals, count, partner, chosen, small):
    core = lax.rem(lax.axis_index("rep"), 2)
    counts = pltpu.make_async_copy(count_hbm, count, small.at[0])
    partners = pltpu.make_async_copy(partner_hbm, partner, small.at[1])
    counts.start()
    partners.start()
    totals[...] = jnp.zeros_like(totals)
    counts.wait()
    partners.wait()

    def visit(some):
        values = []
        for block, slot, live in some:
            row = (partner[block, slot] - FIRST_PHONON) * COMPONENTS
            near, far = mine[pl.ds(row, COMPONENTS), :], other[pl.ds(row, COMPONENTS), :]
            left, right = jnp.where(core == 0, near, far), jnp.where(core == 0, far, near)
            picked = jnp.concatenate([left, right], axis=1)
            padded = jnp.concatenate([picked, jnp.zeros((2, STATES), jnp.float32)], axis=0)
            high, both = stack_split(jnp.where(live, padded, 0.0))
            pair = block * SLOTS + slot
            values.append(multiply(high, both, high_ref[pair], low_ref[pair], 1))
        for (block, slot, live), value in zip(some, values):
            totals[block] += value

    visit_live(count, chosen, None, visit)
    for block in range(BLOCKS):
        own = drag[block * COMPONENTS : (block + 1) * COMPONENTS, :]
        for half in range(2):
            first = half * ROWS + block * COMPONENTS
            value = totals[block, :COMPONENTS, half * HALF : (half + 1) * HALF]
            out[first : first + COMPONENTS, :] = value + jnp.where(core == half, own, 0.0)


VMEM = pl.BlockSpec(memory_space=pltpu.VMEM)
HBM = pl.BlockSpec(memory_space=pltpu.HBM)
HELD = pltpu.VMEM((PAIRS, STATES, STATES), jnp.float32)
LISTS = [
    pltpu.SMEM((1, BLOCKS), jnp.int32),
    pltpu.SMEM((BLOCKS, SLOTS), jnp.int32),
    pltpu.SMEM((PAIRS,), jnp.int32),
]
RATE_SEMS = pltpu.SemaphoreType.DMA((PAIRS,))
SMALL_SEMS = pltpu.SemaphoreType.DMA((2,))


def rate_kernel(body, name, outs, in_specs, scratch):
    return pl.pallas_call(
        body,
        name=name,
        out_shape=outs,
        in_specs=in_specs,
        out_specs=[VMEM] * len(outs),
        scratch_shapes=scratch,
        compiler_params=pltpu.CompilerParams(vmem_limit_bytes=16 * 1024 * 1024),
        cost_estimate=pl.CostEstimate(
            flops=6 * PAIRS * 8 * STATES * STATES,
            bytes_accessed=2 * PAIRS * STATES * STATES * 4,
            transcendentals=0,
        ),
    )


def in_hbm(*values):
    return [pltpu.with_memory_space_constraint(value, pltpu.HBM) for value in values]


def float_rows(rows):
    return jax.ShapeDtypeStruct((rows, HALF), jnp.float32)


def spread(count, partner, deviation, rates):
    own = pltpu.VMEM((COMPONENTS, BLOCKS, STATES), jnp.float32)
    padded = pltpu.VMEM((BLOCKS, 8, STATES), jnp.float32)
    scratch = [own, padded, HELD] + LISTS + [pltpu.SemaphoreType.DMA, RATE_SEMS, SMALL_SEMS]
    return rate_kernel(
        spread_kernel, "spread", [float_rows(PHONON * COMPONENTS)] * 2, [HBM] * 4, scratch
    )(*in_hbm(count, partner, deviation, rates))


def prepare(count, partner, rates):
    terms = [jax.ShapeDtypeStruct((PAIRS, STATES, STATES), jnp.bfloat16)] * 2
    scratch = [HELD] + LISTS + [RATE_SEMS, SMALL_SEMS]
    return rate_kernel(prepare_kernel, "prepare", terms + [float_rows(8)], [HBM] * 3, scratch)(
        *in_hbm(count, partner, rates)
    )


def forward(count, partner, mine, other, high, low, drag):
    totals = pltpu.VMEM((BLOCKS, 8, STATES), jnp.float32)
    return rate_kernel(
        forward_kernel,
        "forward",
        [float_rows(2 * ROWS)],
        [pl.BlockSpec(memory_space=pl.ANY)] * 2 + [VMEM] * 5,
        [totals] + LISTS + [SMALL_SEMS],
    )(count, partner, mine, other, high, low, drag)[0]


def on_device(deviation, source, lifetime, rates, partner, count):
    core = lax.axis_index("rep") % 2
    quarter = lax.axis_index("grp") // OWNERS
    is_phonon = quarter == 3
    live = count.T
    turned = deviation.transpose(1, 0, 2)

    own = lax.dynamic_slice_in_dim(turned, core * HALF, HALF, 2)
    own = own.transpose(1, 0, 2).reshape(1, ROWS, HALF)

    keep, give = spread(live, partner, turned, rates)
    drag = (keep + swap(give, CORE)).reshape(OWNERS, ROWS, HALF)
    half = OWNERS // 2
    drag = jnp.where(quarter % 2 == 1, drag, jnp.concatenate([drag[half:], drag[:half]]))

    parcel = jnp.where(is_phonon, own, drag)
    arrived = lax.all_to_all(parcel, "grp", 0, 0, axis_index_groups=QUARTERS, tiled=True)
    arrived, live = lax.optimization_barrier((arrived, live))
    rates_high, rates_low, token = prepare(live, partner, rates)
    drag = arrived.sum(0)
    gathered = arrived.reshape(PHONON * COMPONENTS, HALF)
    spare = jnp.zeros((PHONON * COMPONENTS - ROWS, HALF), jnp.float32)
    outgoing = jnp.where(is_phonon, gathered, jnp.concatenate([drag, spare]))
    incoming = [swap(outgoing, bits) for bits in (QUARTER_BITS, MIRROR, Y_LO)]
    drag = incoming[0][:ROWS] + incoming[1][:ROWS] + incoming[2][:ROWS]
    phonon = jnp.where(quarter == 0, incoming[0], jnp.where(quarter == 1, incoming[2], incoming[1]))
    phonon = jnp.where(is_phonon, gathered, phonon)
    phonon, token = lax.optimization_barrier((phonon, swap(token, CORE)))
    drag = jnp.where(is_phonon, drag + token[:1], 0.0)
    total = forward(live, partner, phonon, swap(phonon, CORE), rates_high, rates_low, drag)
    total = total + swap(total, CORE)
    total = total + swap(total, Y_HI)
    total = total.reshape(2, BLOCKS, COMPONENTS, HALF)
    summed = jnp.concatenate([total[0], total[1]], axis=-1)
    return source + lifetime[:, None, :] * summed


def solution(mesh):
    placed = (
        P("grp", None, None),
        P("grp", None, None),
        P("grp", None),
        P("grp", "rep", None, None),
        P("grp", "rep"),
        P("grp", "rep"),
    )
    return jax.shard_map(
        on_device, mesh=mesh, in_specs=placed, out_specs=P("grp", None, None), check_vma=False
    )
```

```python
import jax
import jax.numpy as jnp
from jax import lax
from jax.experimental import pallas as pl
from jax.experimental.pallas import tpu as pltpu
from jax.sharding import PartitionSpec as P

Y_LO, X_LOW, Y_HI, CORE = 128, 32, 2, 1
MIRROR = 64 + 32
DEVICES = 256
BLOCKS, SLOTS, COMPONENTS, STATES, HALF = 4, 5, 6, 256, 128
PAIRS = BLOCKS * SLOTS
UNROLL = 4
PHONON = 64
FIRST_PHONON = 192
ROWS = BLOCKS * COMPONENTS
OWNERS = PHONON // BLOCKS
LINE = 8
SAME_X = [[y * 4 * LINE + x * LINE + z for y in range(2) for z in range(LINE)] for x in range(4)]


def swap(value, bit):
    return lax.ppermute(value, ("grp", "rep"), [(i, i ^ bit) for i in range(DEVICES)])


def split(value):
    high = value.astype(jnp.bfloat16)
    low = (value - high.astype(jnp.float32)).astype(jnp.bfloat16)
    return high, low


def stack_split(value):
    high, low = split(value)
    both = jnp.concatenate([high.astype(jnp.float32), low.astype(jnp.float32)], axis=0)
    return high, both.astype(jnp.bfloat16)


def multiply(high, both, rates_high, rates_low, contract):
    dims = (((1,), (contract,)), ((), ()))
    main = lax.dot_general(both, rates_high, dims, preferred_element_type=jnp.float32)
    rest = lax.dot_general(high, rates_low, dims, preferred_element_type=jnp.float32)
    return main[:8] + main[8:] + rest


def product(high, both, weights, contract):
    return multiply(high, both, *split(weights), contract)


def rate_copies(count_hbm, partner_hbm, rates, count, partner, held, sems, small_sems, meanwhile):
    def fetch(block, slot):
        pair = block * SLOTS + slot
        return pltpu.make_async_copy(rates.at[block, slot], held.at[pair], sems.at[pair])

    counts = pltpu.make_async_copy(count_hbm, count, small_sems.at[0])
    partners = pltpu.make_async_copy(partner_hbm, partner, small_sems.at[1])
    counts.start()
    partners.start()
    for block in range(BLOCKS):
        fetch(block, 0).start()
    meanwhile()
    counts.wait()
    for block in range(BLOCKS):

        @pl.loop(1, count[0, block])
        def _(slot):
            fetch(block, slot).start()

    partners.wait()
    return fetch


def visit_live(count, chosen, fetch, visit):
    total = jnp.int32(0)
    for block in range(BLOCKS):

        def note(slot, at):
            chosen[at] = block * SLOTS + slot
            return at + 1

        total = lax.fori_loop(0, count[0, block], note, total)

    @pl.loop(0, lax.div(total + (UNROLL - 1), UNROLL))
    def _(step):
        places = [step * UNROLL + offset for offset in range(UNROLL)]
        pairs = [chosen[jnp.minimum(place, total - 1)] for place in places]
        blocks = [lax.div(pair, SLOTS) for pair in pairs]
        slots = [pair - SLOTS * block for pair, block in zip(pairs, blocks)]
        for place, block, slot in zip(places, blocks, slots):

            if fetch is not None:

                @pl.when(place < total)
                def _():
                    fetch(block, slot).wait()

        visit([(block, slot, place < total) for block, slot, place in zip(blocks, slots, places)])


def spread_kernel(
    count_hbm, partner_hbm, deviation, rates, keep, give, own, rows, held, count, partner, chosen, own_sem, sems, small
):
    core = lax.rem(lax.axis_index("rep"), 2)

    def clear():
        keep[...] = jnp.zeros_like(keep)
        give[...] = jnp.zeros_like(give)

    @pl.when(lax.axis_index("grp") >= 3 * OWNERS)
    def _():
        clear()

    @pl.when(lax.axis_index("grp") < 3 * OWNERS)
    def _():
        own_copy = pltpu.make_async_copy(deviation, own, own_sem)
        own_copy.start()
        fetch = rate_copies(
            count_hbm, partner_hbm, rates, count, partner, held, sems, small, clear
        )
        own_copy.wait()
        for block in range(BLOCKS):
            parts = [own[component, block : block + 1, :] for component in range(COMPONENTS)]
            rows[block] = jnp.concatenate(parts + [jnp.zeros((2, STATES), jnp.float32)], axis=0)

        def visit(some):
            values = []
            for block, slot, live in some:
                high, both = stack_split(jnp.where(live, rows[block], 0.0))
                values.append(product(high, both, held[block * SLOTS + slot], 0)[:COMPONENTS])
            for (block, slot, live), value in zip(some, values):
                left, right = value[:, :HALF], value[:, HALF:]
                row = (partner[block, slot] - FIRST_PHONON) * COMPONENTS
                keep[pl.ds(row, COMPONENTS), :] += jnp.where(core == 0, left, right)
                give[pl.ds(row, COMPONENTS), :] += jnp.where(core == 0, right, left)

        visit_live(count, chosen, fetch, visit)


def prepare_kernel(count_hbm, partner_hbm, rates, high, low, token, held, count, partner, chosen, sems, small):
    def clear():
        token[...] = jnp.zeros_like(token)

    fetch = rate_copies(
        count_hbm, partner_hbm, rates, count, partner, held, sems, small, clear
    )

    def visit(some):
        for block, slot, _ in some:
            pair = block * SLOTS + slot
            high[pair], low[pair] = split(held[pair])

    visit_live(count, chosen, fetch, visit)


def forward_kernel(count_hbm, partner_hbm, mine, other, high_ref, low_ref, drag, out, totals, count, partner, chosen, small):
    core = lax.rem(lax.axis_index("rep"), 2)
    counts = pltpu.make_async_copy(count_hbm, count, small.at[0])
    partners = pltpu.make_async_copy(partner_hbm, partner, small.at[1])
    counts.start()
    partners.start()
    totals[...] = jnp.zeros_like(totals)
    counts.wait()
    partners.wait()

    def visit(some):
        values = []
        for block, slot, live in some:
            row = (partner[block, slot] - FIRST_PHONON) * COMPONENTS
            near, far = mine[pl.ds(row, COMPONENTS), :], other[pl.ds(row, COMPONENTS), :]
            left, right = jnp.where(core == 0, near, far), jnp.where(core == 0, far, near)
            picked = jnp.concatenate([left, right], axis=1)
            padded = jnp.concatenate([picked, jnp.zeros((2, STATES), jnp.float32)], axis=0)
            high, both = stack_split(jnp.where(live, padded, 0.0))
            pair = block * SLOTS + slot
            values.append(multiply(high, both, high_ref[pair], low_ref[pair], 1))
        for (block, slot, live), value in zip(some, values):
            totals[block] += value

    visit_live(count, chosen, None, visit)
    for block in range(BLOCKS):
        own = drag[block * COMPONENTS : (block + 1) * COMPONENTS, :]
        for half in range(2):
            first = half * ROWS + block * COMPONENTS
            value = totals[block, :COMPONENTS, half * HALF : (half + 1) * HALF]
            out[first : first + COMPONENTS, :] = value + jnp.where(core == half, own, 0.0)


VMEM = pl.BlockSpec(memory_space=pltpu.VMEM)
HBM = pl.BlockSpec(memory_space=pltpu.HBM)
HELD = pltpu.VMEM((PAIRS, STATES, STATES), jnp.float32)
LISTS = [
    pltpu.SMEM((1, BLOCKS), jnp.int32),
    pltpu.SMEM((BLOCKS, SLOTS), jnp.int32),
    pltpu.SMEM((PAIRS,), jnp.int32),
]
RATE_SEMS = pltpu.SemaphoreType.DMA((PAIRS,))
SMALL_SEMS = pltpu.SemaphoreType.DMA((2,))


def rate_kernel(body, name, outs, in_specs, scratch):
    return pl.pallas_call(
        body,
        name=name,
        out_shape=outs,
        in_specs=in_specs,
        out_specs=[VMEM] * len(outs),
        scratch_shapes=scratch,
        compiler_params=pltpu.CompilerParams(vmem_limit_bytes=16 * 1024 * 1024),
        cost_estimate=pl.CostEstimate(
            flops=6 * PAIRS * 8 * STATES * STATES,
            bytes_accessed=2 * PAIRS * STATES * STATES * 4,
            transcendentals=0,
        ),
    )


def in_hbm(*values):
    return [pltpu.with_memory_space_constraint(value, pltpu.HBM) for value in values]


def float_rows(rows):
    return jax.ShapeDtypeStruct((rows, HALF), jnp.float32)


def spread(count, partner, deviation, rates):
    own = pltpu.VMEM((COMPONENTS, BLOCKS, STATES), jnp.float32)
    padded = pltpu.VMEM((BLOCKS, 8, STATES), jnp.float32)
    scratch = [own, padded, HELD] + LISTS + [pltpu.SemaphoreType.DMA, RATE_SEMS, SMALL_SEMS]
    return rate_kernel(
        spread_kernel, "spread", [float_rows(PHONON * COMPONENTS)] * 2, [HBM] * 4, scratch
    )(*in_hbm(count, partner, deviation, rates))


def prepare(count, partner, rates):
    terms = [jax.ShapeDtypeStruct((PAIRS, STATES, STATES), jnp.bfloat16)] * 2
    scratch = [HELD] + LISTS + [RATE_SEMS, SMALL_SEMS]
    return rate_kernel(prepare_kernel, "prepare", terms + [float_rows(8)], [HBM] * 3, scratch)(
        *in_hbm(count, partner, rates)
    )


def forward(count, partner, mine, other, high, low, drag):
    totals = pltpu.VMEM((BLOCKS, 8, STATES), jnp.float32)
    return rate_kernel(
        forward_kernel,
        "forward",
        [float_rows(2 * ROWS)],
        [pl.BlockSpec(memory_space=pl.ANY)] * 2 + [VMEM] * 5,
        [totals] + LISTS + [SMALL_SEMS],
    )(count, partner, mine, other, high, low, drag)[0]


def on_device(deviation, source, lifetime, rates, partner, count):
    grp = lax.axis_index("grp")
    core = lax.axis_index("rep") % 2
    x = grp // LINE % 4
    x_high = x >= 2
    outer = (x == 0) | (x == 3)
    is_phonon = x_high & (grp >= 2 * OWNERS)
    live = count.T
    turned = deviation.transpose(1, 0, 2)

    own = lax.dynamic_slice_in_dim(turned, core * HALF, HALF, 2)
    own = own.transpose(1, 0, 2).reshape(1, ROWS, HALF)

    keep, give = spread(live, partner, turned, rates)
    drag = (keep + swap(give, CORE)).reshape(OWNERS, ROWS, HALF)

    drag = jnp.where(outer, drag, jnp.concatenate([drag[LINE:], drag[:LINE]]))
    parcel = jnp.where(is_phonon, own, drag)
    arrived = lax.all_to_all(parcel, "grp", 0, 0, axis_index_groups=SAME_X, tiled=True)
    arrived, live = lax.optimization_barrier((arrived, live))
    rates_high, rates_low, token = prepare(live, partner, rates)
    drag = arrived[:LINE].sum(0) + jnp.where(x_high, 0.0, arrived[LINE:].sum(0))
    line = arrived[LINE:].reshape(LINE * ROWS, HALF)

    spare = jnp.zeros((LINE * ROWS - ROWS, HALF), jnp.float32)
    incoming = swap(jnp.where(x_high, line, jnp.concatenate([drag, spare])), MIRROR)
    line = jnp.where(x_high, line, incoming)
    drag = drag + incoming[:ROWS]

    other = swap(line, X_LOW)
    drag = drag + swap(drag, X_LOW + Y_LO)
    first, second = jnp.where(outer, other, line), jnp.where(outer, line, other)
    phonon = jnp.concatenate([first, second])
    phonon, token = lax.optimization_barrier((phonon, swap(token, CORE)))
    drag = jnp.where(is_phonon, drag + token[:1], 0.0)
    total = forward(live, partner, phonon, swap(phonon, CORE), rates_high, rates_low, drag)
    total = total + swap(total, CORE)
    total = total + swap(total, Y_HI)
    total = total.reshape(2, BLOCKS, COMPONENTS, HALF)
    summed = jnp.concatenate([total[0], total[1]], axis=-1)
    return source + lifetime[:, None, :] * summed


def solution(mesh):
    placed = (
        P("grp", None, None),
        P("grp", None, None),
        P("grp", None),
        P("grp", "rep", None, None),
        P("grp", "rep"),
        P("grp", "rep"),
    )
    return jax.shard_map(
        on_device, mesh=mesh, in_specs=placed, out_specs=P("grp", None, None), check_vma=False
    )
```

```python
import jax
import jax.numpy as jnp
from jax import lax
from jax.experimental import pallas as pl
from jax.experimental.pallas import tpu as pltpu
from jax.sharding import PartitionSpec as P

Y_LO, X_LOW, Y_HI, CORE = 128, 32, 2, 1
MIRROR = 64 + 32
DEVICES = 256
BLOCKS, SLOTS, COMPONENTS, STATES, HALF = 4, 5, 6, 256, 128
PAIRS = BLOCKS * SLOTS
UNROLL = 4
PHONON = 64
FIRST_PHONON = 192
ROWS = BLOCKS * COMPONENTS
OWNERS = PHONON // BLOCKS
LINE = 8
SAME_X = [[y * 4 * LINE + x * LINE + z for y in range(2) for z in range(LINE)] for x in range(4)]


def swap(value, bit):
    return lax.ppermute(value, ("grp", "rep"), [(i, i ^ bit) for i in range(DEVICES)])


def split(value):
    high = value.astype(jnp.bfloat16)
    low = (value - high.astype(jnp.float32)).astype(jnp.bfloat16)
    return high, low


def stack_split(value):
    high, low = split(value)
    both = jnp.concatenate([high.astype(jnp.float32), low.astype(jnp.float32)], axis=0)
    return high, both.astype(jnp.bfloat16)


def multiply(high, both, rates_high, rates_low, contract):
    dims = (((1,), (contract,)), ((), ()))
    main = lax.dot_general(both, rates_high, dims, preferred_element_type=jnp.float32)
    rest = lax.dot_general(high, rates_low, dims, preferred_element_type=jnp.float32)
    return main[:8] + main[8:] + rest


def product(high, both, weights, contract):
    return multiply(high, both, *split(weights), contract)


def rate_copies(count_hbm, partner_hbm, rates, count, partner, held, sems, small_sems, meanwhile):
    def fetch(block, slot):
        pair = block * SLOTS + slot
        return pltpu.make_async_copy(rates.at[block, slot], held.at[pair], sems.at[pair])

    counts = pltpu.make_async_copy(count_hbm, count, small_sems.at[0])
    partners = pltpu.make_async_copy(partner_hbm, partner, small_sems.at[1])
    counts.start()
    partners.start()
    for block in range(BLOCKS):
        fetch(block, 0).start()
    meanwhile()
    counts.wait()
    for block in range(BLOCKS):

        @pl.loop(1, count[0, block])
        def _(slot):
            fetch(block, slot).start()

    partners.wait()
    return fetch


def visit_live(count, chosen, fetch, visit):
    for block in range(BLOCKS):
        chosen[block] = block * SLOTS
    total = jnp.int32(BLOCKS)
    for block in range(BLOCKS):

        def note(slot, at):
            chosen[at] = block * SLOTS + slot
            return at + 1

        total = lax.fori_loop(1, count[0, block], note, total)

    @pl.loop(0, lax.div(total + (UNROLL - 1), UNROLL))
    def _(step):
        places = [step * UNROLL + offset for offset in range(UNROLL)]
        pairs = [chosen[jnp.minimum(place, total - 1)] for place in places]
        blocks = [lax.div(pair, SLOTS) for pair in pairs]
        slots = [pair - SLOTS * block for pair, block in zip(pairs, blocks)]
        for place, block, slot in zip(places, blocks, slots):

            if fetch is not None:

                @pl.when(place < total)
                def _():
                    fetch(block, slot).wait()

        visit([(block, slot, place < total) for block, slot, place in zip(blocks, slots, places)])


def spread_kernel(
    count_hbm, partner_hbm, deviation, rates, keep, give, own, rows, held, count, partner, chosen, own_sem, sems, small
):
    core = lax.rem(lax.axis_index("rep"), 2)

    def clear():
        keep[...] = jnp.zeros_like(keep)
        give[...] = jnp.zeros_like(give)

    @pl.when(lax.axis_index("grp") >= 3 * OWNERS)
    def _():
        clear()

    @pl.when(lax.axis_index("grp") < 3 * OWNERS)
    def _():
        own_copy = pltpu.make_async_copy(deviation, own, own_sem)
        own_copy.start()
        fetch = rate_copies(
            count_hbm, partner_hbm, rates, count, partner, held, sems, small, clear
        )
        own_copy.wait()
        for block in range(BLOCKS):
            parts = [own[component, block : block + 1, :] for component in range(COMPONENTS)]
            rows[block] = jnp.concatenate(parts + [jnp.zeros((2, STATES), jnp.float32)], axis=0)

        def visit(some):
            values = []
            for block, slot, live in some:
                high, both = stack_split(jnp.where(live, rows[block], 0.0))
                values.append(product(high, both, held[block * SLOTS + slot], 0)[:COMPONENTS])
            for (block, slot, live), value in zip(some, values):
                left, right = value[:, :HALF], value[:, HALF:]
                row = (partner[block, slot] - FIRST_PHONON) * COMPONENTS
                keep[pl.ds(row, COMPONENTS), :] += jnp.where(core == 0, left, right)
                give[pl.ds(row, COMPONENTS), :] += jnp.where(core == 0, right, left)

        visit_live(count, chosen, fetch, visit)


def prepare_kernel(count_hbm, partner_hbm, rates, high, low, token, held, count, partner, chosen, sems, small):
    def clear():
        token[...] = jnp.zeros_like(token)

    fetch = rate_copies(
        count_hbm, partner_hbm, rates, count, partner, held, sems, small, clear
    )

    def visit(some):
        for block, slot, _ in some:
            pair = block * SLOTS + slot
            high[pair], low[pair] = split(held[pair])

    visit_live(count, chosen, fetch, visit)


def forward_kernel(count_hbm, partner_hbm, mine, other, high_ref, low_ref, drag, out, totals, count, partner, chosen, small):
    core = lax.rem(lax.axis_index("rep"), 2)
    counts = pltpu.make_async_copy(count_hbm, count, small.at[0])
    partners = pltpu.make_async_copy(partner_hbm, partner, small.at[1])
    counts.start()
    partners.start()
    totals[...] = jnp.zeros_like(totals)
    counts.wait()
    partners.wait()

    def visit(some):
        values = []
        for block, slot, live in some:
            row = (partner[block, slot] - FIRST_PHONON) * COMPONENTS
            near, far = mine[pl.ds(row, COMPONENTS), :], other[pl.ds(row, COMPONENTS), :]
            left, right = jnp.where(core == 0, near, far), jnp.where(core == 0, far, near)
            picked = jnp.concatenate([left, right], axis=1)
            padded = jnp.concatenate([picked, jnp.zeros((2, STATES), jnp.float32)], axis=0)
            high, both = stack_split(jnp.where(live, padded, 0.0))
            pair = block * SLOTS + slot
            values.append(multiply(high, both, high_ref[pair], low_ref[pair], 1))
        for (block, slot, live), value in zip(some, values):
            totals[block] += value

    visit_live(count, chosen, None, visit)
    for block in range(BLOCKS):
        own = drag[block * COMPONENTS : (block + 1) * COMPONENTS, :]
        for half in range(2):
            first = half * ROWS + block * COMPONENTS
            value = totals[block, :COMPONENTS, half * HALF : (half + 1) * HALF]
            out[first : first + COMPONENTS, :] = value + jnp.where(core == half, own, 0.0)


VMEM = pl.BlockSpec(memory_space=pltpu.VMEM)
HBM = pl.BlockSpec(memory_space=pltpu.HBM)
HELD = pltpu.VMEM((PAIRS, STATES, STATES), jnp.float32)
LISTS = [
    pltpu.SMEM((1, BLOCKS), jnp.int32),
    pltpu.SMEM((BLOCKS, SLOTS), jnp.int32),
    pltpu.SMEM((PAIRS,), jnp.int32),
]
RATE_SEMS = pltpu.SemaphoreType.DMA((PAIRS,))
SMALL_SEMS = pltpu.SemaphoreType.DMA((2,))


def rate_kernel(body, name, outs, in_specs, scratch):
    return pl.pallas_call(
        body,
        name=name,
        out_shape=outs,
        in_specs=in_specs,
        out_specs=[VMEM] * len(outs),
        scratch_shapes=scratch,
        compiler_params=pltpu.CompilerParams(vmem_limit_bytes=16 * 1024 * 1024),
        cost_estimate=pl.CostEstimate(
            flops=6 * PAIRS * 8 * STATES * STATES,
            bytes_accessed=2 * PAIRS * STATES * STATES * 4,
            transcendentals=0,
        ),
    )


def in_hbm(*values):
    return [pltpu.with_memory_space_constraint(value, pltpu.HBM) for value in values]


def float_rows(rows):
    return jax.ShapeDtypeStruct((rows, HALF), jnp.float32)


def spread(count, partner, deviation, rates):
    own = pltpu.VMEM((COMPONENTS, BLOCKS, STATES), jnp.float32)
    padded = pltpu.VMEM((BLOCKS, 8, STATES), jnp.float32)
    scratch = [own, padded, HELD] + LISTS + [pltpu.SemaphoreType.DMA, RATE_SEMS, SMALL_SEMS]
    return rate_kernel(
        spread_kernel, "spread", [float_rows(PHONON * COMPONENTS)] * 2, [HBM] * 4, scratch
    )(*in_hbm(count, partner, deviation, rates))


def prepare(count, partner, rates):
    terms = [jax.ShapeDtypeStruct((PAIRS, STATES, STATES), jnp.bfloat16)] * 2
    scratch = [HELD] + LISTS + [RATE_SEMS, SMALL_SEMS]
    return rate_kernel(prepare_kernel, "prepare", terms + [float_rows(8)], [HBM] * 3, scratch)(
        *in_hbm(count, partner, rates)
    )


def forward(count, partner, mine, other, high, low, drag):
    totals = pltpu.VMEM((BLOCKS, 8, STATES), jnp.float32)
    return rate_kernel(
        forward_kernel,
        "forward",
        [float_rows(2 * ROWS)],
        [pl.BlockSpec(memory_space=pl.ANY)] * 2 + [VMEM] * 5,
        [totals] + LISTS + [SMALL_SEMS],
    )(count, partner, mine, other, high, low, drag)[0]


def on_device(deviation, source, lifetime, rates, partner, count):
    grp = lax.axis_index("grp")
    core = lax.axis_index("rep") % 2
    x = grp // LINE % 4
    x_high = x >= 2
    outer = (x == 0) | (x == 3)
    is_phonon = x_high & (grp >= 2 * OWNERS)
    live = count.T
    turned = deviation.transpose(1, 0, 2)

    own = lax.dynamic_slice_in_dim(turned, core * HALF, HALF, 2)
    own = own.transpose(1, 0, 2).reshape(1, ROWS, HALF)

    keep, give = spread(live, partner, turned, rates)
    drag = (keep + swap(give, CORE)).reshape(OWNERS, ROWS, HALF)

    drag = jnp.where(outer, drag, jnp.concatenate([drag[LINE:], drag[:LINE]]))
    parcel = jnp.where(is_phonon, own, drag)
    arrived = lax.all_to_all(parcel, "grp", 0, 0, axis_index_groups=SAME_X, tiled=True)
    arrived, live = lax.optimization_barrier((arrived, live))
    rates_high, rates_low, token = prepare(live, partner, rates)
    drag = arrived[:LINE].sum(0) + jnp.where(x_high, 0.0, arrived[LINE:].sum(0))
    line = arrived[LINE:].reshape(LINE * ROWS, HALF)

    spare = jnp.zeros((LINE * ROWS - ROWS, HALF), jnp.float32)
    incoming = swap(jnp.where(x_high, line, jnp.concatenate([drag, spare])), MIRROR)
    line = jnp.where(x_high, line, incoming)
    drag = drag + incoming[:ROWS]

    other = swap(line, X_LOW)
    drag = drag + swap(drag, X_LOW + Y_LO)
    first, second = jnp.where(outer, other, line), jnp.where(outer, line, other)
    phonon = jnp.concatenate([first, second])
    phonon, token = lax.optimization_barrier((phonon, swap(token, CORE)))
    drag = jnp.where(is_phonon, drag + token[:1], 0.0)
    total = forward(live, partner, phonon, swap(phonon, CORE), rates_high, rates_low, drag)
    total = total + swap(total, CORE)
    total = total + swap(total, Y_HI)
    total = total.reshape(2, BLOCKS, COMPONENTS, HALF).transpose(0, 2, 1, 3)
    summed = jnp.concatenate([total[0], total[1]], axis=-1)
    result = source.transpose(1, 0, 2) + lifetime[None] * summed
    return result.transpose(1, 0, 2)


def solution(mesh):
    placed = (
        P("grp", None, None),
        P("grp", None, None),
        P("grp", None),
        P("grp", "rep", None, None),
        P("grp", "rep"),
        P("grp", "rep"),
    )
    return jax.shard_map(
        on_device, mesh=mesh, in_specs=placed, out_specs=P("grp", None, None), check_vma=False
    )
```

```python
import jax
import jax.numpy as jnp
from jax import lax
from jax.experimental import pallas as pl
from jax.experimental.pallas import tpu as pltpu
from jax.sharding import PartitionSpec as P

Y_LO, X_LOW, Y_HI, CORE = 128, 32, 2, 1
MIRROR = 64 + 32
DEVICES = 256
BLOCKS, SLOTS, COMPONENTS, STATES, HALF = 4, 5, 6, 256, 128
PAIRS = BLOCKS * SLOTS
UNROLL = 4
PHONON = 64
FIRST_PHONON = 192
ROWS = BLOCKS * COMPONENTS
OWNERS = PHONON // BLOCKS
LINE = 8
SAME_X = [[y * 4 * LINE + x * LINE + z for y in range(2) for z in range(LINE)] for x in range(4)]


def swap(value, bit):
    return lax.ppermute(value, ("grp", "rep"), [(i, i ^ bit) for i in range(DEVICES)])


def split(value):
    high = value.astype(jnp.bfloat16)
    low = (value - high.astype(jnp.float32)).astype(jnp.bfloat16)
    return high, low


def stack_split(value):
    high, low = split(value)
    both = jnp.concatenate([high.astype(jnp.float32), low.astype(jnp.float32)], axis=0)
    return high, both.astype(jnp.bfloat16)


def multiply(high, both, rates_high, rates_low, contract):
    dims = (((1,), (contract,)), ((), ()))
    main = lax.dot_general(both, rates_high, dims, preferred_element_type=jnp.float32)
    rest = lax.dot_general(high, rates_low, dims, preferred_element_type=jnp.float32)
    return main[:8] + main[8:] + rest


def product(high, both, weights, contract):
    return multiply(high, both, *split(weights), contract)


def rate_copies(count_hbm, partner_hbm, rates, count, partner, held, sems, small_sems, meanwhile, sure=1):
    def fetch(block, slot):
        pair = block * SLOTS + slot
        return pltpu.make_async_copy(rates.at[block, slot], held.at[pair], sems.at[pair])

    counts = pltpu.make_async_copy(count_hbm, count, small_sems.at[0])
    partners = pltpu.make_async_copy(partner_hbm, partner, small_sems.at[1])
    counts.start()
    partners.start()
    for slot in range(sure):
        for block in range(BLOCKS):
            fetch(block, slot).start()
    meanwhile()
    counts.wait()
    for block in range(BLOCKS):

        @pl.loop(sure, count[0, block])
        def _(slot):
            fetch(block, slot).start()

    partners.wait()
    return fetch


def visit_live(count, chosen, fetch, visit):
    for block in range(BLOCKS):
        chosen[block] = block * SLOTS
    total = jnp.int32(BLOCKS)
    for block in range(BLOCKS):

        def note(slot, at):
            chosen[at] = block * SLOTS + slot
            return at + 1

        total = lax.fori_loop(1, count[0, block], note, total)

    @pl.loop(0, lax.div(total + (UNROLL - 1), UNROLL))
    def _(step):
        places = [step * UNROLL + offset for offset in range(UNROLL)]
        pairs = [chosen[jnp.minimum(place, total - 1)] for place in places]
        blocks = [lax.div(pair, SLOTS) for pair in pairs]
        slots = [pair - SLOTS * block for pair, block in zip(pairs, blocks)]
        for place, block, slot in zip(places, blocks, slots):

            if fetch is not None:

                @pl.when(place < total)
                def _():
                    fetch(block, slot).wait()

        visit([(block, slot, place < total) for block, slot, place in zip(blocks, slots, places)])


def spread_kernel(
    count_hbm, partner_hbm, deviation, rates, keep, give, own, rows, held, count, partner, chosen, own_sem, sems, small
):
    core = lax.rem(lax.axis_index("rep"), 2)

    def clear():
        keep[...] = jnp.zeros_like(keep)
        give[...] = jnp.zeros_like(give)

    @pl.when(lax.axis_index("grp") >= 3 * OWNERS)
    def _():
        clear()

    @pl.when(lax.axis_index("grp") < 3 * OWNERS)
    def _():
        own_copy = pltpu.make_async_copy(deviation, own, own_sem)
        own_copy.start()
        fetch = rate_copies(
            count_hbm, partner_hbm, rates, count, partner, held, sems, small, clear, 2
        )
        own_copy.wait()
        for block in range(BLOCKS):
            parts = [own[component, block : block + 1, :] for component in range(COMPONENTS)]
            rows[block] = jnp.concatenate(parts + [jnp.zeros((2, STATES), jnp.float32)], axis=0)

        def visit(some):
            values = []
            for block, slot, live in some:
                high, both = stack_split(jnp.where(live, rows[block], 0.0))
                values.append(product(high, both, held[block * SLOTS + slot], 0)[:COMPONENTS])
            for (block, slot, live), value in zip(some, values):
                left, right = value[:, :HALF], value[:, HALF:]
                row = (partner[block, slot] - FIRST_PHONON) * COMPONENTS
                keep[pl.ds(row, COMPONENTS), :] += jnp.where(core == 0, left, right)
                give[pl.ds(row, COMPONENTS), :] += jnp.where(core == 0, right, left)

        visit_live(count, chosen, fetch, visit)
        for block in range(BLOCKS):

            @pl.when(count[0, block] < 2)
            def _():
                fetch(block, 1).wait()


def prepare_kernel(count_hbm, partner_hbm, rates, high, low, token, held, count, partner, chosen, sems, small):
    def clear():
        token[...] = jnp.zeros_like(token)

    fetch = rate_copies(
        count_hbm, partner_hbm, rates, count, partner, held, sems, small, clear
    )

    def visit(some):
        for block, slot, _ in some:
            pair = block * SLOTS + slot
            high[pair], low[pair] = split(held[pair])

    visit_live(count, chosen, fetch, visit)


def forward_kernel(count_hbm, partner_hbm, mine, other, high_ref, low_ref, drag, out, totals, count, partner, chosen, small):
    core = lax.rem(lax.axis_index("rep"), 2)
    counts = pltpu.make_async_copy(count_hbm, count, small.at[0])
    partners = pltpu.make_async_copy(partner_hbm, partner, small.at[1])
    counts.start()
    partners.start()
    totals[...] = jnp.zeros_like(totals)
    counts.wait()
    partners.wait()

    def visit(some):
        values = []
        for block, slot, live in some:
            row = (partner[block, slot] - FIRST_PHONON) * COMPONENTS
            near, far = mine[pl.ds(row, COMPONENTS), :], other[pl.ds(row, COMPONENTS), :]
            left, right = jnp.where(core == 0, near, far), jnp.where(core == 0, far, near)
            picked = jnp.concatenate([left, right], axis=1)
            padded = jnp.concatenate([picked, jnp.zeros((2, STATES), jnp.float32)], axis=0)
            high, both = stack_split(jnp.where(live, padded, 0.0))
            pair = block * SLOTS + slot
            values.append(multiply(high, both, high_ref[pair], low_ref[pair], 1))
        for (block, slot, live), value in zip(some, values):
            totals[block] += value

    visit_live(count, chosen, None, visit)
    for block in range(BLOCKS):
        own = drag[block * COMPONENTS : (block + 1) * COMPONENTS, :]
        for half in range(2):
            first = half * ROWS + block * COMPONENTS
            value = totals[block, :COMPONENTS, half * HALF : (half + 1) * HALF]
            out[first : first + COMPONENTS, :] = value + jnp.where(core == half, own, 0.0)


VMEM = pl.BlockSpec(memory_space=pltpu.VMEM)
HBM = pl.BlockSpec(memory_space=pltpu.HBM)
HELD = pltpu.VMEM((PAIRS, STATES, STATES), jnp.float32)
LISTS = [
    pltpu.SMEM((1, BLOCKS), jnp.int32),
    pltpu.SMEM((BLOCKS, SLOTS), jnp.int32),
    pltpu.SMEM((PAIRS,), jnp.int32),
]
RATE_SEMS = pltpu.SemaphoreType.DMA((PAIRS,))
SMALL_SEMS = pltpu.SemaphoreType.DMA((2,))


def rate_kernel(body, name, outs, in_specs, scratch):
    return pl.pallas_call(
        body,
        name=name,
        out_shape=outs,
        in_specs=in_specs,
        out_specs=[VMEM] * len(outs),
        scratch_shapes=scratch,
        compiler_params=pltpu.CompilerParams(vmem_limit_bytes=16 * 1024 * 1024),
        cost_estimate=pl.CostEstimate(
            flops=6 * PAIRS * 8 * STATES * STATES,
            bytes_accessed=2 * PAIRS * STATES * STATES * 4,
            transcendentals=0,
        ),
    )


def in_hbm(*values):
    return [pltpu.with_memory_space_constraint(value, pltpu.HBM) for value in values]


def float_rows(rows):
    return jax.ShapeDtypeStruct((rows, HALF), jnp.float32)


def spread(count, partner, deviation, rates):
    own = pltpu.VMEM((COMPONENTS, BLOCKS, STATES), jnp.float32)
    padded = pltpu.VMEM((BLOCKS, 8, STATES), jnp.float32)
    scratch = [own, padded, HELD] + LISTS + [pltpu.SemaphoreType.DMA, RATE_SEMS, SMALL_SEMS]
    return rate_kernel(
        spread_kernel, "spread", [float_rows(PHONON * COMPONENTS)] * 2, [HBM] * 4, scratch
    )(*in_hbm(count, partner, deviation, rates))


def prepare(count, partner, rates):
    terms = [jax.ShapeDtypeStruct((PAIRS, STATES, STATES), jnp.bfloat16)] * 2
    scratch = [HELD] + LISTS + [RATE_SEMS, SMALL_SEMS]
    return rate_kernel(prepare_kernel, "prepare", terms + [float_rows(8)], [HBM] * 3, scratch)(
        *in_hbm(count, partner, rates)
    )


def forward(count, partner, mine, other, high, low, drag):
    totals = pltpu.VMEM((BLOCKS, 8, STATES), jnp.float32)
    return rate_kernel(
        forward_kernel,
        "forward",
        [float_rows(2 * ROWS)],
        [pl.BlockSpec(memory_space=pl.ANY)] * 2 + [VMEM] * 5,
        [totals] + LISTS + [SMALL_SEMS],
    )(count, partner, mine, other, high, low, drag)[0]


def on_device(deviation, source, lifetime, rates, partner, count):
    grp = lax.axis_index("grp")
    core = lax.axis_index("rep") % 2
    x = grp // LINE % 4
    x_high = x >= 2
    outer = (x == 0) | (x == 3)
    is_phonon = x_high & (grp >= 2 * OWNERS)
    live = count.T
    turned = deviation.transpose(1, 0, 2)

    own = lax.dynamic_slice_in_dim(turned, core * HALF, HALF, 2)
    own = own.transpose(1, 0, 2).reshape(1, ROWS, HALF)

    keep, give = spread(live, partner, turned, rates)
    drag = (keep + swap(give, CORE)).reshape(OWNERS, ROWS, HALF)

    drag = jnp.where(outer, drag, jnp.concatenate([drag[LINE:], drag[:LINE]]))
    parcel = jnp.where(is_phonon, own, drag)
    arrived = lax.all_to_all(parcel, "grp", 0, 0, axis_index_groups=SAME_X, tiled=True)
    arrived, live = lax.optimization_barrier((arrived, live))
    rates_high, rates_low, token = prepare(live, partner, rates)
    drag = arrived[:LINE].sum(0) + jnp.where(x_high, 0.0, arrived[LINE:].sum(0))
    line = arrived[LINE:].reshape(LINE * ROWS, HALF)

    spare = jnp.zeros((LINE * ROWS - ROWS, HALF), jnp.float32)
    incoming = swap(jnp.where(x_high, line, jnp.concatenate([drag, spare])), MIRROR)
    line = jnp.where(x_high, line, incoming)
    drag = drag + incoming[:ROWS]

    other = swap(line, X_LOW)
    drag = drag + swap(drag, X_LOW + Y_LO)
    first, second = jnp.where(outer, other, line), jnp.where(outer, line, other)
    phonon = jnp.concatenate([first, second])
    phonon, token = lax.optimization_barrier((phonon, swap(token, CORE)))
    drag = jnp.where(is_phonon, drag + token[:1], 0.0)
    total = forward(live, partner, phonon, swap(phonon, CORE), rates_high, rates_low, drag)
    total = total + swap(total, CORE)
    total = total + swap(total, Y_HI)
    total = total.reshape(2, BLOCKS, COMPONENTS, HALF).transpose(0, 2, 1, 3)
    summed = jnp.concatenate([total[0], total[1]], axis=-1)
    result = source.transpose(1, 0, 2) + lifetime[None] * summed
    return result.transpose(1, 0, 2)


def solution(mesh):
    placed = (
        P("grp", None, None),
        P("grp", None, None),
        P("grp", None),
        P("grp", "rep", None, None),
        P("grp", "rep"),
        P("grp", "rep"),
    )
    return jax.shard_map(
        on_device, mesh=mesh, in_specs=placed, out_specs=P("grp", None, None), check_vma=False
    )
```
